512 devices in a mesh: head: 8 (over y, x_lo), outer: 16 (over z), inner: 4 (over x_hi, core).
Axes of the slice: x: 4 (x_hi: 2, x_lo: 2; x = x_hi * 2 + x_lo), y: 4, z: 16, core: 2. Of those that a mesh axis runs over, the one named last changes fastest.
Arguments:
- queries: bfloat16 [4096, 8192], P('outer', ('head', 'inner')), may hold values from -100 to 100
- keys: bfloat16 [4096, 1024], P('outer', 'head'), may hold values from -5 to 5
- values: bfloat16 [4096, 1024], P('outer', 'head'), may hold values from -6 to 6
- grad_out: bfloat16 [4096, 8192], P('outer', ('head', 'inner')), may hold values from -24 to 24
- hidden_in: bfloat16 [4096, 8192], P('outer', ('head', 'inner')), may hold values from -6 to 6
- adapter_a: bfloat16 [8192, 16], P(('head', 'inner')), may hold values from -0.0625 to 0.0625
- adapter_b: bfloat16 [16, 1024], P(None, 'head'), may hold values from -1.5 to 1.5
- block_order: int32 [32], replicated, may hold values from 0 to 31, each once
- doc_ids: int32 [4096], replicated, may hold values from 0 to 3, never falling along the last dimension, each value on 1 to 2048 neighbouring positions
Outputs:
- grad_query: bfloat16 [4096, 8192], P('outer', ('head', 'inner'))
- grad_key: bfloat16 [4096, 1024], P('outer', 'head')
- grad_value: bfloat16 [4096, 1024], P('outer', 'head')
- grad_a: float32 [8192, 16], P(('head', 'inner'))
- grad_b: float32 [16, 1024], P(None, 'head')
The draws below stay inside these ranges and needn't reach their ends.
Inputs may be any that keep to these rules, and one draw needn't show every extreme that they name: `block_order`: a permutation of the stored blocks. `doc_ids`: never falling along positions; each document has 1 to 2048 positions.
All inputs are finite; a program needn't handle non-finite values.
Results may differ from the reference program's by a relative error of at most 0.024.
Values may be sent and summed in bfloat16 or wider, within the bound.
No kernel may reach another device: no remote copies, remote signals or barrier semaphores. Data moves between devices by JAX's collectives and lax.ppermute only.
A program may use at most 64 MiB of HBM per device.

```python
import math
import jax
import jax.numpy as jnp
import numpy as np
from jax import lax

D = 8192
HEAD_DIM = 128
GROUP = 8
RANK = 16
DOCS = 4
TOK_DEV = 256
KV_HEADS = 8
SEQ = 4096
NBLK = 32


def drawn_pair(key):
    base_key = jax.random.fold_in(key, 11)
    key_one, key_two = jax.random.split(base_key, 2)
    query_draw = jax.random.truncated_normal(key_one, -4.5, 4.5, (SEQ, KV_HEADS * GROUP * HEAD_DIM), jnp.float32)
    key_draw = jax.random.truncated_normal(key_two, -4.5, 4.5, (SEQ, KV_HEADS * HEAD_DIM), jnp.float32)
    return (query_draw, key_draw)


def draw_queries(key, part):
    return drawn_pair(key)[0].astype(jnp.bfloat16)


def draw_keys(key, part):
    return drawn_pair(key)[1].astype(jnp.bfloat16)


def shard_levels(key, dims, cuts, smallest, top_value):
    loudness = 1.0
    for dim, parts in cuts:
        steps = jax.random.uniform(jax.random.fold_in(jax.random.fold_in(key, 6), dim), (parts,), jnp.float32, smallest / len(cuts), top_value / len(cuts))
        loudness = loudness * jnp.repeat(jnp.exp(steps), dims[dim] // parts).reshape((-1,) + (1,) * (len(dims) - 1 - dim))
    return loudness


def profile(number_of, total, bound, lean):
    portions = [(1 << 20) // math.isqrt(grade ** lean) + 1 for grade in range(2, number_of + 1)]
    rest, holding = total - bound - (number_of - 1), [1] * (number_of - 1)
    while rest > 0:
        movable = [i for i in range(number_of - 1) if holding[i] < bound]
        pool, left = sum([portions[i] for i in movable]), rest
        for i in movable:
            addition = min(bound - holding[i], max(1, left * portions[i] // pool), rest)
            holding[i] = holding[i] + addition
            rest = rest - addition
    return np.array([bound] + holding)


def ragged(rng, amount, total, bound, lean):
    if amount == 2:
        one = jax.random.randint(rng, (), max(1, total - bound), min(bound, total - 1) + 1)
        return jnp.stack([one, total - one])
    sizes = jnp.asarray(profile(amount, total, bound, lean), jnp.int32)
    couples = (amount - 1) // 2
    source_of, taker = sizes[1:1 + 2 * couples:2], sizes[2:2 + 2 * couples:2]
    margin = jnp.minimum(source_of - 1, bound - taker)
    shifted = jax.random.randint(jax.random.fold_in(rng, 1), (couples,), 0, 1 << 20) % (margin + 1)
    sizes = sizes.at[1:1 + 2 * couples:2].set(source_of - shifted).at[2:2 + 2 * couples:2].set(taker + shifted)
    return sizes[jax.random.permutation(jax.random.fold_in(rng, 2), amount)]


def noise(stream_key, extent, width, limit, cuts=(), kind=jnp.bfloat16):
    factor_of = shard_levels(stream_key, extent, cuts, -0.22, 0.18) if cuts else 1.0
    values = jax.random.normal(stream_key, extent, jnp.float32) * width * factor_of
    return jnp.minimum(jnp.maximum(values, -limit), limit).astype(kind)


def setup_inputs(seed: int = 0) -> dict:
    streams_of = jax.random.split(jax.random.key(seed), 10)
    return {
        "queries": draw_queries(jax.random.fold_in(streams_of[9], 71), 0),
        "keys": draw_keys(jax.random.fold_in(streams_of[9], 71), 0),
        "values": noise(streams_of[2], (SEQ, KV_HEADS * HEAD_DIM), 1.0, 6.0, ((0, 16), (1, 8))),
        "grad_out": noise(streams_of[3], (SEQ, KV_HEADS * GROUP * HEAD_DIM), 4.0, 24.0, ((0, 16), (1, 32))),
        "hidden_in": noise(streams_of[4], (SEQ, D), 1.0, 6.0, ((0, 16), (1, 32))),
        "adapter_a": noise(streams_of[5], (D, RANK), D ** -0.5, 0.0625, ((0, 32),)),
        "adapter_b": noise(streams_of[6], (RANK, KV_HEADS * HEAD_DIM), RANK ** -0.5, 1.5, ((1, 8),)),
        "block_order": jax.random.permutation(streams_of[7], NBLK).astype(jnp.int32),
        "doc_ids": jnp.searchsorted(jnp.cumsum(ragged(streams_of[8], DOCS, SEQ, SEQ // 2, 2)), jnp.arange(SEQ), side="right").astype(jnp.int32),
    }


NEGATIVE = -1.0e30


def rounded(values_in):
    return lax.optimization_barrier(values_in.astype(jnp.bfloat16)).astype(jnp.float32)


def head_pass(query_head, key_head, value_head, grad_head, places, owners):
    total_rows = key_head.shape[0]
    length = min(512, total_rows)
    scaling = HEAD_DIM ** -0.5
    keys_wide = key_head.astype(jnp.float32)
    values_wide = value_head.astype(jnp.float32)

    def block_step(carried, first_row):
        grad_key, grad_value = carried
        query_blk = lax.dynamic_slice_in_dim(query_head, first_row, length, 0).astype(jnp.float32)
        grad_blk = lax.dynamic_slice_in_dim(grad_head, first_row, length, 0).astype(jnp.float32)
        q_places = lax.dynamic_slice_in_dim(places, first_row, length, 0)
        q_owners = lax.dynamic_slice_in_dim(owners, first_row, length, 0)
        masked = (places[None, :] <= q_places[:, None]) & (owners[None, :] == q_owners[:, None])
        scores = jnp.einsum("tgd,sd->gts", query_blk, keys_wide) * scaling
        scores = jnp.where(masked[None], scores, NEGATIVE)
        peak_score = jnp.max(scores, axis=-1)
        weights = jnp.where(masked[None], jnp.exp(scores - peak_score[..., None]), 0.0)
        totals = jnp.sum(weights, axis=-1)
        output = jnp.einsum("gts,sd->gtd", rounded(weights), values_wide) / totals[..., None]
        lse_rows = peak_score + jnp.log(totals)
        delta_rows = jnp.sum(output * jnp.transpose(grad_blk, (1, 0, 2)), axis=-1)
        prob_tile = jnp.where(masked[None], jnp.exp(scores - lse_rows[..., None]), 0.0)
        grad_value = grad_value + jnp.einsum("gts,tgd->sd", rounded(prob_tile), grad_blk)
        dot_tile = jnp.einsum("tgd,sd->gts", grad_blk, values_wide)
        slopes = rounded(prob_tile * (dot_tile - delta_rows[..., None]))
        grad_query = jnp.einsum("gts,sd->tgd", slopes, keys_wide) * scaling
        grad_key = grad_key + jnp.einsum("gts,tgd->sd", slopes, query_blk)
        return (grad_key, grad_value), grad_query.astype(jnp.bfloat16)

    starts = jnp.arange(0, total_rows, length, dtype=jnp.int32)
    empty_rows = jnp.zeros((total_rows, HEAD_DIM), jnp.float32)
    (grad_key, grad_value), grad_query = lax.scan(block_step, (empty_rows, empty_rows), starts)
    grad_query = grad_query.reshape(total_rows, GROUP, HEAD_DIM)
    return grad_query, (grad_key * scaling).astype(jnp.bfloat16), grad_value.astype(jnp.bfloat16)


def reference(queries, keys, values, grad_out, hidden_in, adapter_a, adapter_b, block_order, doc_ids):
    total_rows = queries.shape[0]
    half_rows = TOK_DEV // 2
    kv_heads = keys.shape[1] // HEAD_DIM
    places = (block_order[:, None] * half_rows + jnp.arange(half_rows, dtype=jnp.int32)[None, :]).reshape(-1).astype(jnp.int32)
    owners = jnp.take(doc_ids, places).astype(jnp.int32)
    query_heads = jnp.transpose(queries.reshape(total_rows, kv_heads, GROUP, HEAD_DIM), (1, 0, 2, 3))
    grad_heads = jnp.transpose(grad_out.reshape(total_rows, kv_heads, GROUP, HEAD_DIM), (1, 0, 2, 3))
    key_heads = jnp.transpose(keys.reshape(total_rows, kv_heads, HEAD_DIM), (1, 0, 2))
    value_heads = jnp.transpose(values.reshape(total_rows, kv_heads, HEAD_DIM), (1, 0, 2))

    def one_head(packed):
        return head_pass(packed[0], packed[1], packed[2], packed[3], places, owners)

    grad_q, grad_k, grad_v = lax.map(one_head, (query_heads, key_heads, value_heads, grad_heads))
    grad_query = jnp.transpose(grad_q, (1, 0, 2, 3)).reshape(total_rows, -1)
    grad_key = jnp.transpose(grad_k, (1, 0, 2)).reshape(total_rows, -1)
    grad_value = jnp.transpose(grad_v, (1, 0, 2)).reshape(total_rows, -1)
    low_rank = jnp.dot(hidden_in, adapter_a, preferred_element_type=jnp.float32).astype(jnp.bfloat16)
    back_rank = lax.dot_general(grad_key, adapter_b, (((1,), (1,)), ((), ())), preferred_element_type=jnp.float32).astype(jnp.bfloat16)
    grad_a = lax.dot_general(hidden_in, back_rank, (((0,), (0,)), ((), ())), preferred_element_type=jnp.float32)
    grad_b = lax.dot_general(low_rank, grad_key, (((0,), (0,)), ((), ())), preferred_element_type=jnp.float32)
    return grad_query, grad_key, grad_value, grad_a, grad_b
```

```python
import functools

import jax
import jax.numpy as jnp
from jax import lax
from jax.experimental import pallas as pl
from jax.experimental.pallas import tpu as pltpu
from jax.sharding import PartitionSpec as P

HEAD_DIM = 128
SCALE = HEAD_DIM ** (-0.5)
LOG2E = 1.4426950408889634
HIDDEN_SCORE = -2e30
LOWEST = -1e30
CHUNK = 128
DOCS = 4
VMEM_BYTES = 48 * 1024 * 1024
bf16 = jnp.bfloat16
f32 = jnp.float32


def nt(a, b):
    return lax.dot_general(a, b, (((1,), (1,)), ((), ())), preferred_element_type=f32)


def nn(a, b):
    return lax.dot_general(a, b, (((1,), (0,)), ((), ())), preferred_element_type=f32)


def tn(a, b):
    return lax.dot_general(a, b, (((0,), (0,)), ((), ())), preferred_element_type=f32)


def stage(meta, qg, kv, qs, gs, kvs, part):
    sources, rows, width = qg.shape
    half = rows // 2
    grp = width // 2 // HEAD_DIM
    for t in range(2):
        for i in range(sources):
            for g in range(grp):
                at = (i * grp + g) * half
                qs[t, at : at + half, :] = qg[i, t * half : (t + 1) * half, g * HEAD_DIM : (g + 1) * HEAD_DIM]
                gs[t, at : at + half, :] = qg[
                    i, t * half : (t + 1) * half, (grp + g) * HEAD_DIM : (grp + g + 1) * HEAD_DIM
                ]
    for b in range(kv.shape[0] // part):
        to = pl.multiple_of(meta[2 + b] * part, part)
        kvs[pl.ds(to, part), :] = kv[b * part : (b + 1) * part, :]


def block_rows(meta, docs, t, part):
    half = docs.shape[1]
    block = meta[2 + 2 * meta[1] + t]
    own = docs[pl.ds(block, 1), :]
    table = docs[...]
    first = jnp.zeros_like(own)
    for d in range(DOCS - 1):
        ones = (table == d).astype(jnp.int32)
        count = jnp.sum(jnp.sum(ones, axis=0, keepdims=True), axis=1, keepdims=True)
        first = first + jnp.where(own > d, count, 0)
    places = block * half + lax.broadcasted_iota(jnp.int32, (1, half), 1)
    low = (jnp.min(first) // half) * part // CHUNK
    high = (block * part + part - 1) // CHUNK + 1
    return places, first, low, high


def chunk_bias(meta, places, first, c, part, heads):
    half = places.shape[1]
    n = c * CHUNK + lax.broadcasted_iota(jnp.int32, (CHUNK, half), 0)
    keys = (n // part) * half + part * meta[0] + n % part
    seen = (keys <= places) & (keys >= first)
    bias = jnp.where(seen, 0.0, HIDDEN_SCORE)
    return jnp.concatenate([bias] * heads, axis=1)


def forward_kernel(part, meta, docs, qg, kv, stats, qs, gs, kvs):
    stage(meta, qg, kv, qs, gs, kvs, part)
    columns = qs.shape[1]
    heads = columns // docs.shape[1]
    stats[...] = jnp.zeros_like(stats)
    for t in range(2):
        places, first, low, high = block_rows(meta, docs, t, part)

        def body(c, carried, t=t, places=places, first=first):
            peak, total, dot = carried
            at = pl.multiple_of(c * CHUNK, CHUNK)
            k = kvs[pl.ds(at, CHUNK), :HEAD_DIM]
            v = kvs[pl.ds(at, CHUNK), HEAD_DIM:]
            s = nt(k, qs[t]) * (SCALE * LOG2E) + chunk_bias(meta, places, first, c, part, heads)
            dp = nt(v, gs[t])
            new = jnp.maximum(peak, jnp.max(s, axis=0, keepdims=True))
            w = jnp.exp2(s - new)
            factor = jnp.exp2(peak - new)
            total = total * factor + jnp.sum(w, axis=0, keepdims=True)
            dot = dot * factor + jnp.sum(w * dp, axis=0, keepdims=True)
            return new, total, dot

        zero = jnp.zeros((1, columns), f32)
        peak, total, dot = lax.fori_loop(low, high, body, (zero + LOWEST, zero, zero))
        span = slice(t * columns, (t + 1) * columns)
        stats[0:1, span] = peak
        stats[1:2, span] = total
        stats[2:3, span] = dot


def backward_kernel(part, meta, docs, qg, kv, stats, dq, dkv, qs, gs, kvs, acc, dqt):
    stage(meta, qg, kv, qs, gs, kvs, part)
    columns = qs.shape[1]
    half = docs.shape[1]
    heads = columns // half
    sources = stats.shape[0]
    grp = heads // sources
    acc[...] = jnp.zeros_like(acc)
    for t in range(2):
        places, first, low, high = block_rows(meta, docs, t, part)
        span = slice(t * columns, (t + 1) * columns)
        peaks = [stats[i, 0:1, span] for i in range(sources)]
        peak = functools.reduce(jnp.maximum, peaks)
        factors = [jnp.exp2(p - peak) for p in peaks]
        total = sum(stats[i, 1:2, span] * factors[i] for i in range(sources))
        dot = sum(stats[i, 2:3, span] * factors[i] for i in range(sources))
        lse = peak + jnp.log2(total)
        delta = dot / total
        dqt[...] = jnp.zeros_like(dqt)

        def body(c, carried, t=t, places=places, first=first, lse=lse, delta=delta):
            at = pl.multiple_of(c * CHUNK, CHUNK)
            k = kvs[pl.ds(at, CHUNK), :HEAD_DIM]
            v = kvs[pl.ds(at, CHUNK), HEAD_DIM:]
            s = nt(k, qs[t]) * (SCALE * LOG2E) + chunk_bias(meta, places, first, c, part, heads)
            p = jnp.exp2(s - lse)
            dp = nt(v, gs[t])
            ds = (p * (dp - delta)).astype(bf16)
            acc[pl.ds(at, CHUNK), :HEAD_DIM] += nn(ds, qs[t])
            acc[pl.ds(at, CHUNK), HEAD_DIM:] += nn(p.astype(bf16), gs[t])
            dqt[...] += tn(k, ds)
            return carried

        lax.fori_loop(low, high, body, 0)
        for h in range(heads):
            i, g = divmod(h, grp)
            dq[i, t * half : (t + 1) * half, g * HEAD_DIM : (g + 1) * HEAD_DIM] = (
                dqt[:, h * half : (h + 1) * half].T.astype(bf16)
            )
    for b in range(kv.shape[0] // part):
        at = pl.multiple_of(meta[2 + b] * part, part)
        dkv[b * part : (b + 1) * part, :] = acc[pl.ds(at, part), :].astype(bf16)


def home_kernel(parts, low, ab, dkv, payload):
    total = parts[0].astype(f32)
    for o in range(1, parts.shape[0]):
        total = total + parts[o].astype(f32)
    rows = total.shape[0]
    dk = (total[:, :HEAD_DIM] * SCALE).astype(bf16)
    dkv[:, :HEAD_DIM] = dk
    dkv[:, HEAD_DIM:] = total[:, HEAD_DIM:].astype(bf16)
    back = nt(ab[...], dk).astype(bf16)
    low_rank = low[0]
    for o in range(1, low.shape[0]):
        low_rank = low_rank + low[o]
    gb = nn(low_rank.astype(bf16), dk).astype(bf16)
    whole = jnp.concatenate([back, jnp.zeros((back.shape[0], HEAD_DIM - rows), bf16), gb], axis=1)
    for o in range(payload.shape[0]):
        payload[o] = whole


def adapter_kernel(inner_size, meta, parts, hidden, payload):
    heads = parts.shape[0] // inner_size
    rows = hidden.shape[0] // inner_size
    piece = rows // 2
    half = hidden.shape[0] // 2
    ga = None
    gb = None
    for i in range(inner_size):
        back = parts[i].astype(f32)
        for h in range(1, heads):
            back = back + parts[h * inner_size + i].astype(f32)
        mine = jnp.concatenate(
            [hidden[i * piece : (i + 1) * piece, :], hidden[half + i * piece : half + (i + 1) * piece, :]], axis=0
        )
        term = nn(back[:, :rows].astype(bf16), mine)
        ga = term if ga is None else ga + term
        own = parts[meta[0] * inner_size + i].astype(f32)[:, HEAD_DIM:]
        gb = own if gb is None else gb + own
    whole = jnp.concatenate([ga, gb], axis=1).astype(bf16)
    for o in range(payload.shape[0]):
        payload[o] = whole


def final_kernel(parts, ga, gb):
    total = parts[0].astype(f32)
    for o in range(1, parts.shape[0]):
        total = total + parts[o].astype(f32)
    width = ga.shape[0]
    ga[...] = total[:, :width].T
    gb[...] = total[:, width:]


def call(kernel, out_shape, specs, scratch=(), cost=None):
    spaces = {"s": pltpu.SMEM, "v": pltpu.VMEM}
    single = not isinstance(out_shape, tuple)
    return pl.pallas_call(
        kernel,
        out_shape=out_shape,
        in_specs=[pl.BlockSpec(memory_space=spaces[s]) for s in specs],
        out_specs=pl.BlockSpec(memory_space=pltpu.VMEM)
        if single
        else tuple(pl.BlockSpec(memory_space=pltpu.VMEM) for _ in out_shape),
        scratch_shapes=list(scratch),
        compiler_params=pltpu.CompilerParams(vmem_limit_bytes=VMEM_BYTES),
        cost_estimate=cost,
    )


def on_device(queries, keys, values, grad_out, hidden_in, adapter_a, adapter_b, block_order, doc_ids):
    sd = jax.ShapeDtypeStruct
    n_outer, n_inner, n_head = lax.axis_size("outer"), lax.axis_size("inner"), lax.axis_size("head")
    outer, inner, head = lax.axis_index("outer"), lax.axis_index("inner"), lax.axis_index("head")
    tokens = queries.shape[0]
    half = tokens // 2
    part = half // n_inner
    rows = 2 * part
    heads = n_inner * queries.shape[1] // HEAD_DIM
    columns = heads * half
    total_rows = n_outer * rows
    rank = adapter_b.shape[0]

    kv = jnp.concatenate([keys, values], axis=1).reshape(2, n_inner, part, 2 * HEAD_DIM)
    kv = lax.dynamic_index_in_dim(kv, inner, 1, keepdims=False).reshape(rows, 2 * HEAD_DIM)
    qg = jnp.concatenate([queries, grad_out], axis=1)
    qg = lax.all_to_all(jnp.broadcast_to(qg[None], (n_inner, *qg.shape)), "inner", 0, 0, tiled=True)
    kv = lax.all_gather(kv, "outer", axis=0, tiled=True)
    meta = jnp.concatenate([jnp.stack([inner, outer]).astype(jnp.int32), block_order])
    docs = doc_ids.reshape(-1, half)

    low = lax.dot_general(adapter_a, hidden_in, (((0,), (1,)), ((), ())), preferred_element_type=f32)
    low = low.reshape(rank, 2, n_inner, part).transpose(2, 0, 1, 3).reshape(n_inner, rank, rows)
    low = jnp.broadcast_to(low[None], (n_head, n_inner, rank, rows)).reshape(n_head * n_inner, rank, rows)
    low = lax.all_to_all(low, ("head", "inner"), 0, 0, tiled=True)

    staged = [
        pltpu.VMEM((2, columns, HEAD_DIM), bf16),
        pltpu.VMEM((2, columns, HEAD_DIM), bf16),
        pltpu.VMEM((total_rows, 2 * HEAD_DIM), bf16),
    ]
    pair = 2 * columns * total_rows * HEAD_DIM
    stats = call(
        functools.partial(forward_kernel, part),
        sd((4, 2 * columns), f32),
        "svvv",
        staged,
        pl.CostEstimate(flops=2 * pair, bytes_accessed=2 << 20, transcendentals=columns * total_rows),
    )(meta, docs, qg, kv)
    stats = lax.all_gather(stats, "inner", axis=0, tiled=False)
    dq, dkv = call(
        functools.partial(backward_kernel, part),
        (sd((n_inner, tokens, queries.shape[1]), bf16), sd((total_rows, 2 * HEAD_DIM), bf16)),
        "svvvv",
        staged + [pltpu.VMEM((total_rows, 2 * HEAD_DIM), f32), pltpu.VMEM((HEAD_DIM, columns), f32)],
        pl.CostEstimate(flops=5 * pair, bytes_accessed=3 << 20, transcendentals=columns * total_rows),
    )(meta, docs, qg, kv, stats)

    dkv = lax.all_to_all(dkv.reshape(n_outer, rows, 2 * HEAD_DIM), "outer", 0, 0, tiled=True)
    dq = lax.all_to_all(dq, "inner", 0, 0, tiled=True)
    grad_query = (jnp.sum(dq.astype(f32), axis=0) * SCALE).astype(bf16)

    dkv, payload = call(
        home_kernel,
        (sd((rows, 2 * HEAD_DIM), bf16), sd((n_head * n_inner, rank, 2 * HEAD_DIM), bf16)),
        "vvv",
    )(dkv, low, adapter_b)
    payload = lax.all_to_all(payload, ("head", "inner"), 0, 0, tiled=True)
    width = hidden_in.shape[1]
    payload = call(
        functools.partial(adapter_kernel, n_inner), sd((n_outer, rank, width + HEAD_DIM), bf16), "svv"
    )(head.astype(jnp.int32)[None], payload, hidden_in)
    payload = lax.all_to_all(payload, "outer", 0, 0, tiled=True)
    grad_a, grad_b = call(final_kernel, (sd((width, rank), f32), sd((rank, HEAD_DIM), f32)), "v")(payload)

    dkv = lax.all_gather(dkv, "inner", axis=0, tiled=True)
    dkv = dkv.reshape(n_inner, 2, part, 2 * HEAD_DIM).transpose(1, 0, 2, 3).reshape(tokens, 2 * HEAD_DIM)
    return grad_query, dkv[:, :HEAD_DIM], dkv[:, HEAD_DIM:], grad_a, grad_b


def solution(mesh):
    in_specs = (
        P("outer", ("head", "inner")),
        P("outer", "head"),
        P("outer", "head"),
        P("outer", ("head", "inner")),
        P("outer", ("head", "inner")),
        P(("head", "inner"), None),
        P(None, "head"),
        P(),
        P(),
    )
    out_specs = (
        P("outer", ("head", "inner")),
        P("outer", "head"),
        P("outer", "head"),
        P(("head", "inner"), None),
        P(None, "head"),
    )
    return jax.shard_map(on_device, mesh=mesh, in_specs=in_specs, out_specs=out_specs, check_vma=False)
```

```python
import functools

import jax
import jax.numpy as jnp
from jax import lax
from jax.experimental import pallas as pl
from jax.experimental.pallas import tpu as pltpu
from jax.sharding import PartitionSpec as P

HEAD_DIM = 128
SCALE = HEAD_DIM ** (-0.5)
LOG2E = 1.4426950408889634
HIDDEN_SCORE = -2e30
LOWEST = -1e30
CHUNK = 128
DOCS = 4
VMEM_BYTES = 48 * 1024 * 1024
bf16 = jnp.bfloat16
f32 = jnp.float32


def nt(a, b):
    return lax.dot_general(a, b, (((1,), (1,)), ((), ())), preferred_element_type=f32)


def nn(a, b):
    return lax.dot_general(a, b, (((1,), (0,)), ((), ())), preferred_element_type=f32)


def tn(a, b):
    return lax.dot_general(a, b, (((0,), (0,)), ((), ())), preferred_element_type=f32)


def stage(order, q, g, kv, qs, gs, kvs, part):
    sources, tokens, width = q.shape
    half = tokens // 2
    grp = width // HEAD_DIM
    for t in range(2):
        for i in range(sources):
            for n in range(grp):
                at = (i * grp + n) * half
                span = slice(n * HEAD_DIM, (n + 1) * HEAD_DIM)
                qs[t, at : at + half, :] = q[i, t * half : (t + 1) * half, span]
                gs[t, at : at + half, :] = g[i, t * half : (t + 1) * half, span]
    for b in range(kv.shape[0] // part):
        to = pl.multiple_of(order[b] * part, part)
        kvs[pl.ds(to, part), :] = kv[b * part : (b + 1) * part, :]


def block_rows(order, outer, docs, t, part):
    half = docs.shape[1]
    block = order[2 * outer[0] + t]
    own = docs[pl.ds(block, 1), :]
    table = docs[...]
    first = jnp.zeros_like(own)
    for d in range(DOCS - 1):
        ones = (table == d).astype(jnp.int32)
        count = jnp.sum(jnp.sum(ones, axis=0, keepdims=True), axis=1, keepdims=True)
        first = first + jnp.where(own > d, count, 0)
    places = block * half + lax.broadcasted_iota(jnp.int32, (1, half), 1)
    low = (jnp.min(first) // half) * part // CHUNK
    high = (block * part + part - 1) // CHUNK + 1
    return places, first, low, high


def chunk_bias(inner, places, first, c, part, heads):
    half = places.shape[1]
    n = c * CHUNK + lax.broadcasted_iota(jnp.int32, (CHUNK, half), 0)
    keys = (n // part) * half + part * inner[0] + n % part
    seen = (keys <= places) & (keys >= first)
    bias = jnp.where(seen, 0.0, HIDDEN_SCORE)
    return jnp.concatenate([bias] * heads, axis=1)


def forward_kernel(part, inner, outer, order, docs, q, g, kv, lows, stats, low, qs, gs, kvs):
    stage(order, q, g, kv, qs, gs, kvs, part)
    columns = qs.shape[1]
    heads = columns // docs.shape[1]
    stats[...] = jnp.zeros_like(stats)
    whole = lows[0].astype(f32)
    for i in range(1, lows.shape[0]):
        whole = whole + lows[i].astype(f32)
    half = docs.shape[1]
    shift = (half - part * inner[0]) % half
    mine = [pltpu.roll(whole[:, t * half : (t + 1) * half], shift, 1)[:, :part] for t in range(2)]
    low[...] = jnp.concatenate(mine, axis=1)
    for t in range(2):
        places, first, low_chunk, high = block_rows(order, outer, docs, t, part)

        def body(c, carried, t=t, places=places, first=first):
            peak, total, dot = carried
            at = pl.multiple_of(c * CHUNK, CHUNK)
            k = kvs[pl.ds(at, CHUNK), :HEAD_DIM]
            v = kvs[pl.ds(at, CHUNK), HEAD_DIM:]
            s = nt(k, qs[t]) * (SCALE * LOG2E) + chunk_bias(inner, places, first, c, part, heads)
            dp = nt(v, gs[t])
            new = jnp.maximum(peak, jnp.max(s, axis=0, keepdims=True))
            w = jnp.exp2(s - new)
            factor = jnp.exp2(peak - new)
            total = total * factor + jnp.sum(w, axis=0, keepdims=True)
            dot = dot * factor + jnp.sum(w * dp, axis=0, keepdims=True)
            return new, total, dot

        zero = jnp.zeros((1, columns), f32)
        peak, total, dot = lax.fori_loop(low_chunk, high, body, (zero + LOWEST, zero, zero))
        span = slice(t * columns, (t + 1) * columns)
        stats[0:1, span] = peak
        stats[1:2, span] = total
        stats[2:3, span] = dot


def row_terms(stats, t, columns):
    sources = stats.shape[0]
    span = slice(t * columns, (t + 1) * columns)
    peaks = [stats[i, 0:1, span] for i in range(sources)]
    peak = functools.reduce(jnp.maximum, peaks)
    factors = [jnp.exp2(p - peak) for p in peaks]
    total = sum(stats[i, 1:2, span] * factors[i] for i in range(sources))
    dot = sum(stats[i, 2:3, span] * factors[i] for i in range(sources))
    return peak + jnp.log2(total), dot / total


def key_kernel(part, inner, outer, order, docs, q, g, kv, stats, dkv, qs, gs, kvs, acc):
    stage(order, q, g, kv, qs, gs, kvs, part)
    columns = qs.shape[1]
    heads = columns // docs.shape[1]
    acc[...] = jnp.zeros_like(acc)
    for t in range(2):
        places, first, low_chunk, high = block_rows(order, outer, docs, t, part)
        lse, delta = row_terms(stats, t, columns)

        def body(c, carried, t=t, places=places, first=first, lse=lse, delta=delta):
            at = pl.multiple_of(c * CHUNK, CHUNK)
            k = kvs[pl.ds(at, CHUNK), :HEAD_DIM]
            v = kvs[pl.ds(at, CHUNK), HEAD_DIM:]
            s = nt(k, qs[t]) * (SCALE * LOG2E) + chunk_bias(inner, places, first, c, part, heads)
            p = jnp.exp2(s - lse)
            ds = (p * (nt(v, gs[t]) - delta)).astype(bf16)
            acc[pl.ds(at, CHUNK), :HEAD_DIM] += nn(ds, qs[t])
            acc[pl.ds(at, CHUNK), HEAD_DIM:] += nn(p.astype(bf16), gs[t])
            return carried

        lax.fori_loop(low_chunk, high, body, 0)
    for z in range(dkv.shape[0]):
        for t in range(2):
            at = pl.multiple_of(order[2 * z + t] * part, part)
            dkv[z, t * part : (t + 1) * part, :] = acc[pl.ds(at, part), :].astype(bf16)


def query_kernel(part, inner, outer, order, docs, q, g, kv, stats, dq, qs, gs, kvs, dqt):
    stage(order, q, g, kv, qs, gs, kvs, part)
    columns = qs.shape[1]
    half = docs.shape[1]
    heads = columns // half
    grp = heads // stats.shape[0]
    for t in range(2):
        places, first, low_chunk, high = block_rows(order, outer, docs, t, part)
        lse, delta = row_terms(stats, t, columns)
        dqt[...] = jnp.zeros_like(dqt)

        def body(c, carried, t=t, places=places, first=first, lse=lse, delta=delta):
            at = pl.multiple_of(c * CHUNK, CHUNK)
            k = kvs[pl.ds(at, CHUNK), :HEAD_DIM]
            v = kvs[pl.ds(at, CHUNK), HEAD_DIM:]
            s = nt(k, qs[t]) * (SCALE * LOG2E) + chunk_bias(inner, places, first, c, part, heads)
            dqt[...] += tn(k, (jnp.exp2(s - lse) * (nt(v, gs[t]) - delta)).astype(bf16))
            return carried

        lax.fori_loop(low_chunk, high, body, 0)
        for h in range(heads):
            i, n = divmod(h, grp)
            dq[i, t * half : (t + 1) * half, n * HEAD_DIM : (n + 1) * HEAD_DIM] = (
                dqt[:, h * half : (h + 1) * half].T.astype(bf16)
            )


def spread_kernel(part, inner, keys, values, kv, held, arrived):
    half = keys.shape[0] // 2
    copies = []
    for t in range(2):
        here = pl.multiple_of(t * half + inner[0] * part, part)
        for n, source in enumerate((keys, values)):
            copy = pltpu.make_async_copy(
                source.at[pl.ds(here, part), :],
                held.at[t * part : (t + 1) * part, n * HEAD_DIM : (n + 1) * HEAD_DIM],
                arrived.at[2 * t + n],
            )
            copy.start()
            copies.append(copy)
    for copy in copies:
        copy.wait()
    whole = held[...]
    for o in range(kv.shape[0]):
        kv[o] = whole


def home_kernel(parts, ab, low, dkv, payload):
    total = parts[0].astype(f32)
    for o in range(1, parts.shape[0]):
        total = total + parts[o].astype(f32)
    dk = (total[:, :HEAD_DIM] * SCALE).astype(bf16)
    dkv[:, :HEAD_DIM] = dk
    dkv[:, HEAD_DIM:] = total[:, HEAD_DIM:].astype(bf16)
    back = nt(ab[...], dk)
    rank, rows = back.shape
    whole = jnp.concatenate([back, low[...]], axis=1).astype(bf16)
    for o in range(payload.shape[0]):
        payload[o] = whole


def adapter_kernel(inner_size, parts, dkv, hidden, payload):
    heads = parts.shape[0] // inner_size
    rows = hidden.shape[0] // inner_size
    piece = rows // 2
    half = hidden.shape[0] // 2
    ga = None
    gb = None
    for i in range(inner_size):
        both = parts[i].astype(f32)
        for h in range(1, heads):
            both = both + parts[h * inner_size + i].astype(f32)
        both = both.astype(bf16)
        here, there = i * piece, half + i * piece
        mine = jnp.concatenate([hidden[here : here + piece, :], hidden[there : there + piece, :]], axis=0)
        term = nn(both[:, :rows], mine)
        ga = term if ga is None else ga + term
        term = nn(both[:, rows:], dkv[i * rows : (i + 1) * rows, :HEAD_DIM])
        gb = term if gb is None else gb + term
    whole = jnp.concatenate([ga, gb], axis=1).astype(bf16)
    for o in range(payload.shape[0]):
        payload[o] = whole


def final_kernel(parts, ga, gb):
    total = parts[0].astype(f32)
    for o in range(1, parts.shape[0]):
        total = total + parts[o].astype(f32)
    width = ga.shape[1]
    ga[...] = total[:, :width]
    gb[...] = total[:, width:]


def call(kernel, out_shape, specs, scratch=(), cost=None, vmem=VMEM_BYTES):
    spaces = {"s": pltpu.SMEM, "v": pltpu.VMEM, "h": pltpu.HBM}
    single = not isinstance(out_shape, tuple)
    return pl.pallas_call(
        kernel,
        out_shape=out_shape,
        in_specs=[pl.BlockSpec(memory_space=spaces[s]) for s in specs],
        out_specs=pl.BlockSpec(memory_space=pltpu.VMEM)
        if single
        else tuple(pl.BlockSpec(memory_space=pltpu.VMEM) for _ in out_shape),
        scratch_shapes=list(scratch),
        compiler_params=pltpu.CompilerParams(vmem_limit_bytes=vmem),
        cost_estimate=cost,
    )


def on_device(queries, keys, values, grad_out, hidden_in, adapter_a, adapter_b, block_order, doc_ids):
    sd = jax.ShapeDtypeStruct
    n_outer, n_inner, n_head = lax.axis_size("outer"), lax.axis_size("inner"), lax.axis_size("head")
    outer, inner = lax.axis_index("outer"), lax.axis_index("inner")
    tokens = queries.shape[0]
    half = tokens // 2
    part = half // n_inner
    rows = 2 * part
    heads = n_inner * queries.shape[1] // HEAD_DIM
    columns = heads * half
    total_rows = n_outer * rows
    rank = adapter_b.shape[0]

    width = hidden_in.shape[1]
    ids = (inner.astype(jnp.int32)[None], outer.astype(jnp.int32)[None])
    docs = doc_ids.reshape(-1, half)
    kv = call(
        functools.partial(spread_kernel, part),
        sd((n_outer, rows, 2 * HEAD_DIM), bf16),
        "shh",
        [pltpu.VMEM((rows, 2 * HEAD_DIM), bf16), pltpu.SemaphoreType.DMA((4,))],
        vmem=None,
    )(ids[0], keys, values)
    kv = lax.all_to_all(kv, "outer", 0, 0, tiled=True)
    q = lax.all_gather(queries, "inner", axis=0, tiled=False)
    g = lax.all_gather(grad_out, "inner", axis=0, tiled=False)
    lows = lax.all_gather(nt(adapter_a.T, hidden_in).astype(bf16), "inner", axis=0, tiled=False)
    kv, q, g, lows = lax.optimization_barrier((kv, q, g, lows))
    kv = kv.reshape(total_rows, 2 * HEAD_DIM)

    staged = [
        pltpu.VMEM((2, columns, HEAD_DIM), bf16),
        pltpu.VMEM((2, columns, HEAD_DIM), bf16),
        pltpu.VMEM((total_rows, 2 * HEAD_DIM), bf16),
    ]
    pair = 2 * columns * total_rows * HEAD_DIM
    stats, low = call(
        functools.partial(forward_kernel, part),
        (sd((4, 2 * columns), f32), sd((rank, rows), f32)),
        "sssvvvvv",
        staged,
        pl.CostEstimate(flops=2 * pair, bytes_accessed=2 << 20, transcendentals=columns * total_rows),
    )(*ids, block_order, docs, q, g, kv, lows)
    stats = lax.all_gather(stats, "inner", axis=0, tiled=False)
    dkv = call(
        functools.partial(key_kernel, part),
        sd((n_outer, rows, 2 * HEAD_DIM), bf16),
        "sssvvvvv",
        staged + [pltpu.VMEM((total_rows, 2 * HEAD_DIM), f32)],
        pl.CostEstimate(flops=4 * pair, bytes_accessed=3 << 20, transcendentals=columns * total_rows),
    )(*ids, block_order, docs, q, g, kv, stats)
    dkv, stats = lax.optimization_barrier((dkv, stats))
    dq = call(
        functools.partial(query_kernel, part),
        sd((n_inner, tokens, queries.shape[1]), bf16),
        "sssvvvvv",
        staged + [pltpu.VMEM((HEAD_DIM, columns), f32)],
        pl.CostEstimate(flops=3 * pair, bytes_accessed=3 << 20, transcendentals=columns * total_rows),
    )(*ids, block_order, docs, q, g, kv, stats)

    home = lax.all_to_all(dkv, "outer", 0, 0, tiled=True)
    own = lax.dynamic_index_in_dim(dq, inner, 0, keepdims=False).astype(f32)
    for d in range(1, n_inner):
        sent = lax.dynamic_index_in_dim(dq, inner ^ d, 0, keepdims=False)
        own = own + lax.ppermute(sent, "inner", [(i, i ^ d) for i in range(n_inner)]).astype(f32)
    grad_query = (own * SCALE).astype(bf16)

    home, grad_query = lax.optimization_barrier((home, grad_query))
    dkv, payload = call(
        home_kernel,
        (sd((rows, 2 * HEAD_DIM), bf16), sd((n_head * n_inner, rank, 2 * rows), bf16)),
        "vvv",
    )(home, adapter_b, low)
    payload = lax.all_to_all(payload, ("head", "inner"), 0, 0, tiled=True)
    dkv = lax.all_gather(dkv, "inner", axis=0, tiled=True)
    payload = call(
        functools.partial(adapter_kernel, n_inner), sd((n_outer, rank, width + HEAD_DIM), bf16), "vvv"
    )(payload, dkv, hidden_in)
    payload = lax.all_to_all(payload, "outer", 0, 0, tiled=True)

    dkv = dkv.reshape(n_inner, 2, part, 2 * HEAD_DIM).transpose(1, 0, 2, 3).reshape(tokens, 2 * HEAD_DIM)
    grad_key, grad_value = dkv[:, :HEAD_DIM], dkv[:, HEAD_DIM:]
    payload, grad_query, grad_key, grad_value = lax.optimization_barrier(
        (payload, grad_query, grad_key, grad_value)
    )
    grad_a, grad_b = call(final_kernel, (sd((rank, width), f32), sd((rank, HEAD_DIM), f32)), "v")(payload)
    return grad_query, grad_key, grad_value, grad_a.T, grad_b


def solution(mesh):
    in_specs = (
        P("outer", ("head", "inner")),
        P("outer", "head"),
        P("outer", "head"),
        P("outer", ("head", "inner")),
        P("outer", ("head", "inner")),
        P(("head", "inner"), None),
        P(None, "head"),
        P(),
        P(),
    )
    out_specs = (
        P("outer", ("head", "inner")),
        P("outer", "head"),
        P("outer", "head"),
        P(("head", "inner"), None),
        P(None, "head"),
    )
    return jax.shard_map(on_device, mesh=mesh, in_specs=in_specs, out_specs=out_specs, check_vma=False)
```

```python
import functools

import jax
import jax.numpy as jnp
from jax import lax
from jax.experimental import pallas as pl
from jax.experimental.pallas import tpu as pltpu
from jax.sharding import PartitionSpec as P

HEAD_DIM = 128
SCALE = HEAD_DIM ** (-0.5)
LOG2E = 1.4426950408889634
HIDDEN_SCORE = -2e30
LOWEST = -1e30
CHUNK = 256
DOCS = 4
VMEM_BYTES = 48 * 1024 * 1024
bf16 = jnp.bfloat16
f32 = jnp.float32


def nt(a, b):
    return lax.dot_general(a, b, (((1,), (1,)), ((), ())), preferred_element_type=f32)


def nn(a, b):
    return lax.dot_general(a, b, (((1,), (0,)), ((), ())), preferred_element_type=f32)


def tn(a, b):
    return lax.dot_general(a, b, (((0,), (0,)), ((), ())), preferred_element_type=f32)


def sort_keys(order, kv, kvs, part):
    for b in range(kv.shape[0] // part):
        to = pl.multiple_of(order[b] * part, part)
        kvs[pl.ds(to, part), :] = kv[b * part : (b + 1) * part, :]


def stacked(qg, t, half, which):
    sources, _, width = qg.shape
    rows = slice((2 * which + t) * half, (2 * which + t + 1) * half)
    return jnp.concatenate(
        [qg[i, rows, n : n + HEAD_DIM] for i in range(sources) for n in range(0, width, HEAD_DIM)], axis=0
    )


def block_rows(outer, order, docs, t, part):
    half = docs.shape[1]
    block = order[2 * outer[0] + t]
    own = docs[pl.ds(block, 1), :]
    table = docs[...]
    first = jnp.zeros_like(own)
    for d in range(DOCS - 1):
        ones = (table == d).astype(jnp.int32)
        count = jnp.sum(jnp.sum(ones, axis=0, keepdims=True), axis=1, keepdims=True)
        first = first + jnp.where(own > d, count, 0)
    places = block * half + lax.broadcasted_iota(jnp.int32, (1, half), 1)
    low = (jnp.min(first) // half) * part // CHUNK
    high = (block * part + part - 1) // CHUNK + 1
    return places, first, low, high


def chunk_bias(inner, places, first, c, part, heads):
    half = places.shape[1]
    n = c * CHUNK + lax.broadcasted_iota(jnp.int32, (CHUNK, half), 0)
    keys = (n // part) * half + part * inner[0] + n % part
    seen = (keys <= places) & (keys >= first)
    bias = jnp.where(seen, 0.0, HIDDEN_SCORE)
    return jnp.concatenate([bias] * heads, axis=1)


def forward_kernel(part, inner, outer, order, docs, qg, kv, stats, low, kvs):
    sort_keys(order, kv, kvs, part)
    both = [block_rows(outer, order, docs, t, part) for t in range(2)]
    half = docs.shape[1]
    columns = stats.shape[-1] // 2
    heads = columns // half
    stats[...] = jnp.zeros_like(stats)
    rank, rows = low.shape
    total_low = qg[0, qg.shape[1] - rank :, :HEAD_DIM].astype(f32)
    for i in range(1, qg.shape[0]):
        total_low = total_low + qg[i, qg.shape[1] - rank :, :HEAD_DIM].astype(f32)
    low[...] = total_low[:, :rows]
    for t in range(2):
        places, first, low_chunk, high = both[t]

        def body(c, carried, t=t, places=places, first=first):
            peak, total, dot = carried
            at = pl.multiple_of(c * CHUNK, CHUNK)
            k = kvs[pl.ds(at, CHUNK), :HEAD_DIM]
            v = kvs[pl.ds(at, CHUNK), HEAD_DIM:]
            s = nt(k, stacked(qg, t, half, 0)) * (SCALE * LOG2E) + chunk_bias(inner, places, first, c, part, heads)
            dp = nt(v, stacked(qg, t, half, 1))
            new = jnp.maximum(peak, jnp.max(s, axis=0, keepdims=True))
            w = jnp.exp2(s - new)
            factor = jnp.exp2(peak - new)
            total = total * factor + jnp.sum(w, axis=0, keepdims=True)
            dot = dot * factor + jnp.sum(w * dp, axis=0, keepdims=True)
            return new, total, dot

        zero = jnp.zeros((1, columns), f32)
        peak, total, dot = lax.fori_loop(low_chunk, high, body, (zero + LOWEST, zero, zero))
        span = slice(t * columns, (t + 1) * columns)
        stats[0:1, span] = peak
        stats[1:2, span] = total
        stats[2:3, span] = dot


def row_terms(stats, t, columns):
    sources = stats.shape[0]
    span = slice(t * columns, (t + 1) * columns)
    peaks = [stats[i, 0:1, span] for i in range(sources)]
    peak = functools.reduce(jnp.maximum, peaks)
    factors = [jnp.exp2(p - peak) for p in peaks]
    total = sum(stats[i, 1:2, span] * factors[i] for i in range(sources))
    dot = sum(stats[i, 2:3, span] * factors[i] for i in range(sources))
    return peak + jnp.log2(total), dot / total


def key_kernel(part, inner, outer, order, docs, qg, kv, stats, dkv, kvs, acc):
    sort_keys(order, kv, kvs, part)
    both = [block_rows(outer, order, docs, t, part) for t in range(2)]
    half = docs.shape[1]
    columns = stats.shape[-1] // 2
    heads = columns // half
    acc[...] = jnp.zeros_like(acc)
    for t in range(2):
        places, first, low_chunk, high = both[t]
        lse, delta = row_terms(stats, t, columns)

        def body(c, carried, t=t, places=places, first=first, lse=lse, delta=delta):
            at = pl.multiple_of(c * CHUNK, CHUNK)
            k = kvs[pl.ds(at, CHUNK), :HEAD_DIM]
            v = kvs[pl.ds(at, CHUNK), HEAD_DIM:]
            s = nt(k, stacked(qg, t, half, 0)) * (SCALE * LOG2E) + chunk_bias(inner, places, first, c, part, heads)
            p = jnp.exp2(s - lse)
            ds = (p * (nt(v, stacked(qg, t, half, 1)) - delta)).astype(bf16)
            acc[pl.ds(at, CHUNK), :HEAD_DIM] += nn(ds, stacked(qg, t, half, 0))
            acc[pl.ds(at, CHUNK), HEAD_DIM:] += nn(p.astype(bf16), stacked(qg, t, half, 1))
            return carried

        lax.fori_loop(low_chunk, high, body, 0)
    for z in range(dkv.shape[0]):
        for t in range(2):
            at = pl.multiple_of(order[2 * z + t] * part, part)
            dkv[z, t * part : (t + 1) * part, :] = acc[pl.ds(at, part), :].astype(bf16)


def query_kernel(part, inner, outer, order, docs, qg, kv, stats, dq, kvs, dqt):
    sort_keys(order, kv, kvs, part)
    both = [block_rows(outer, order, docs, t, part) for t in range(2)]
    half = docs.shape[1]
    columns = stats.shape[-1] // 2
    heads = columns // half
    grp = heads // stats.shape[0]
    for t in range(2):
        places, first, low_chunk, high = both[t]
        lse, delta = row_terms(stats, t, columns)
        dqt[...] = jnp.zeros_like(dqt)

        def body(c, carried, t=t, places=places, first=first, lse=lse, delta=delta):
            at = pl.multiple_of(c * CHUNK, CHUNK)
            k = kvs[pl.ds(at, CHUNK), :HEAD_DIM]
            v = kvs[pl.ds(at, CHUNK), HEAD_DIM:]
            s = nt(k, stacked(qg, t, half, 0)) * (SCALE * LOG2E) + chunk_bias(inner, places, first, c, part, heads)
            dqt[...] += tn(k, (jnp.exp2(s - lse) * (nt(v, stacked(qg, t, half, 1)) - delta)).astype(bf16))
            return carried

        lax.fori_loop(low_chunk, high, body, 0)
        for h in range(heads):
            i, n = divmod(h, grp)
            dq[i, t * half : (t + 1) * half, n * HEAD_DIM : (n + 1) * HEAD_DIM] = (
                dqt[:, h * half : (h + 1) * half].T.astype(bf16)
            )


def input_kernel(
    part, inner, hidden_, at_, queries, grad_out, keys, values, qg, kv, hidden, at, low, wide, mixed, arrived
):
    sources, _, width = qg.shape
    tokens = queries.shape[0]
    half = tokens // 2
    pairs = [(queries, wide.at[:tokens, :]), (grad_out, wide.at[tokens:, :]), (hidden_, hidden), (at_, at)]
    for t in range(2):
        here = pl.multiple_of(t * half + inner[0] * part, part)
        to = slice(t * part, (t + 1) * part)
        pairs += [(keys.at[pl.ds(here, part), :], mixed.at[to, :HEAD_DIM])]
        pairs += [(values.at[pl.ds(here, part), :], mixed.at[to, HEAD_DIM:])]
    copies = [pltpu.make_async_copy(source, target, arrived.at[n]) for n, (source, target) in enumerate(pairs)]
    for copy in copies:
        copy.start()
    for copy in copies:
        copy.wait()
    pairs = [(wide, qg.at[i, : 2 * tokens, :]) for i in range(sources)] + [(mixed, kv)]
    last = [
        pltpu.make_async_copy(source, target, arrived.at[len(copies) + n]) for n, (source, target) in enumerate(pairs)
    ]
    for copy in last:
        copy.start()
    whole = nt(at[...], hidden[...])
    empty = jnp.zeros((whole.shape[0], width - 2 * part), f32)
    for i in range(sources):
        mine = [whole[:, t * half + i * part : t * half + (i + 1) * part] for t in range(2)]
        low[i] = jnp.concatenate(mine + [empty], axis=1).astype(bf16)
    for i in range(sources):
        copy = pltpu.make_async_copy(low.at[i], qg.at[i, 2 * tokens :, :], arrived.at[len(copies) + len(pairs) + i])
        copy.start()
        last.append(copy)
    for copy in last:
        copy.wait()


def home_kernel(parts, ab, low, dkv, payload):
    total = parts[0].astype(f32)
    for o in range(1, parts.shape[0]):
        total = total + parts[o].astype(f32)
    dk = (total[:, :HEAD_DIM] * SCALE).astype(bf16)
    dkv[:, :HEAD_DIM] = dk
    dkv[:, HEAD_DIM:] = total[:, HEAD_DIM:].astype(bf16)
    back = nt(ab[...], dk)
    rank, rows = back.shape
    whole = jnp.concatenate([back, low[...]], axis=1).astype(bf16)
    for o in range(payload.shape[0]):
        payload[o] = whole


def adapter_kernel(inner_size, parts, dkv, hidden, payload):
    heads = parts.shape[0] // inner_size
    rows = hidden.shape[0] // inner_size
    piece = rows // 2
    half = hidden.shape[0] // 2
    ga = None
    gb = None
    for i in range(inner_size):
        both = parts[i].astype(f32)
        for h in range(1, heads):
            both = both + parts[h * inner_size + i].astype(f32)
        both = both.astype(bf16)
        here, there = i * piece, half + i * piece
        mine = jnp.concatenate([hidden[here : here + piece, :], hidden[there : there + piece, :]], axis=0)
        term = nn(both[:, :rows], mine)
        ga = term if ga is None else ga + term
        term = nn(both[:, rows:], dkv[i * rows : (i + 1) * rows, :HEAD_DIM])
        gb = term if gb is None else gb + term
    whole = jnp.concatenate([ga, gb], axis=1).astype(bf16)
    for o in range(payload.shape[0]):
        payload[o] = whole


def final_kernel(parts, ga, gb):
    total = parts[0].astype(f32)
    for o in range(1, parts.shape[0]):
        total = total + parts[o].astype(f32)
    width = ga.shape[1]
    ga[...] = total[:, :width]
    gb[...] = total[:, width:]


def call(kernel, out_shape, specs, scratch=(), cost=None, vmem=VMEM_BYTES, outs=None):
    spaces = {"s": pltpu.SMEM, "v": pltpu.VMEM, "h": pltpu.HBM}
    single = not isinstance(out_shape, tuple)
    return pl.pallas_call(
        kernel,
        out_shape=out_shape,
        in_specs=[pl.BlockSpec(memory_space=spaces[s]) for s in specs],
        out_specs=pl.BlockSpec(memory_space=pltpu.VMEM)
        if single
        else tuple(pl.BlockSpec(memory_space=spaces[o]) for o in outs or "v" * len(out_shape)),
        scratch_shapes=list(scratch),
        compiler_params=pltpu.CompilerParams(vmem_limit_bytes=vmem),
        cost_estimate=cost,
    )


def on_device(queries, keys, values, grad_out, hidden_in, adapter_a, adapter_b, block_order, doc_ids):
    sd = jax.ShapeDtypeStruct
    n_outer, n_inner, n_head = lax.axis_size("outer"), lax.axis_size("inner"), lax.axis_size("head")
    outer, inner = lax.axis_index("outer"), lax.axis_index("inner")
    tokens = queries.shape[0]
    half = tokens // 2
    part = half // n_inner
    rows = 2 * part
    heads = n_inner * queries.shape[1] // HEAD_DIM
    columns = heads * half
    total_rows = n_outer * rows
    rank = adapter_b.shape[0]

    width = hidden_in.shape[1]
    docs = doc_ids.reshape(-1, half)
    ids = (inner.astype(jnp.int32)[None], outer.astype(jnp.int32)[None], block_order)
    qg, kv = call(
        functools.partial(input_kernel, part),
        (
            sd((n_inner, 2 * tokens + rank, queries.shape[1]), bf16),
            sd((rows, 2 * HEAD_DIM), bf16),
        ),
        "shhhhhh",
        [
            pltpu.VMEM(hidden_in.shape, bf16),
            pltpu.VMEM((rank, width), bf16),
            pltpu.VMEM((n_inner, rank, queries.shape[1]), bf16),
            pltpu.VMEM((2 * tokens, queries.shape[1]), bf16),
            pltpu.VMEM((rows, 2 * HEAD_DIM), bf16),
            pltpu.SemaphoreType.DMA((9 + 2 * n_inner,)),
        ],
        vmem=None,
        outs="hh",
    )(ids[0], hidden_in, adapter_a.T, queries, grad_out, keys, values)
    qg = lax.all_to_all(qg, "inner", 0, 0, tiled=True)
    kv = lax.all_gather(kv, "outer", axis=0, tiled=True)

    staged = [
        pltpu.VMEM((total_rows, 2 * HEAD_DIM), bf16),
    ]
    pair = 2 * columns * total_rows * HEAD_DIM
    stats, low = call(
        functools.partial(forward_kernel, part),
        (sd((4, 2 * columns), f32), sd((rank, rows), f32)),
        "sssvvv",
        staged,
        pl.CostEstimate(flops=2 * pair, bytes_accessed=2 << 20, transcendentals=columns * total_rows),
    )(*ids, docs, qg, kv)
    stats = lax.all_gather(stats, "inner", axis=0, tiled=False)
    dkv = call(
        functools.partial(key_kernel, part),
        sd((n_outer, rows, 2 * HEAD_DIM), bf16),
        "sssvvvv",
        staged + [pltpu.VMEM((total_rows, 2 * HEAD_DIM), f32)],
        pl.CostEstimate(flops=4 * pair, bytes_accessed=3 << 20, transcendentals=columns * total_rows),
    )(*ids, docs, qg, kv, stats)
    dkv, stats = lax.optimization_barrier((dkv, stats))
    dq = call(
        functools.partial(query_kernel, part),
        sd((n_inner, tokens, queries.shape[1]), bf16),
        "sssvvvv",
        staged + [pltpu.VMEM((HEAD_DIM, columns), f32)],
        pl.CostEstimate(flops=3 * pair, bytes_accessed=3 << 20, transcendentals=columns * total_rows),
    )(*ids, docs, qg, kv, stats)

    home = lax.all_to_all(dkv, "outer", 0, 0, tiled=True)
    own = lax.dynamic_index_in_dim(dq, inner, 0, keepdims=False).astype(f32)
    for d in range(1, n_inner):
        sent = lax.dynamic_index_in_dim(dq, inner ^ d, 0, keepdims=False)
        own = own + lax.ppermute(sent, "inner", [(i, i ^ d) for i in range(n_inner)]).astype(f32)
    grad_query = (own * SCALE).astype(bf16)

    home, grad_query = lax.optimization_barrier((home, grad_query))
    dkv, payload = call(
        home_kernel,
        (sd((rows, 2 * HEAD_DIM), bf16), sd((n_head * n_inner, rank, 2 * rows), bf16)),
        "vvv",
    )(home, adapter_b, low)
    payload = lax.all_to_all(payload, ("head", "inner"), 0, 0, tiled=True)
    dkv = lax.all_gather(dkv, "inner", axis=0, tiled=True)
    payload = call(
        functools.partial(adapter_kernel, n_inner), sd((n_outer, rank, width + HEAD_DIM), bf16), "vvv"
    )(payload, dkv, hidden_in)
    payload = lax.all_to_all(payload, "outer", 0, 0, tiled=True)

    dkv = dkv.reshape(n_inner, 2, part, 2 * HEAD_DIM).transpose(1, 0, 2, 3).reshape(tokens, 2 * HEAD_DIM)
    grad_key, grad_value = dkv[:, :HEAD_DIM], dkv[:, HEAD_DIM:]
    payload, grad_query, grad_key, grad_value = lax.optimization_barrier(
        (payload, grad_query, grad_key, grad_value)
    )
    grad_a, grad_b = call(final_kernel, (sd((rank, width), f32), sd((rank, HEAD_DIM), f32)), "v")(payload)
    return grad_query, grad_key, grad_value, grad_a.T, grad_b


def solution(mesh):
    in_specs = (
        P("outer", ("head", "inner")),
        P("outer", "head"),
        P("outer", "head"),
        P("outer", ("head", "inner")),
        P("outer", ("head", "inner")),
        P(("head", "inner"), None),
        P(None, "head"),
        P(),
        P(),
    )
    out_specs = (
        P("outer", ("head", "inner")),
        P("outer", "head"),
        P("outer", "head"),
        P(("head", "inner"), None),
        P(None, "head"),
    )
    return jax.shard_map(on_device, mesh=mesh, in_specs=in_specs, out_specs=out_specs, check_vma=False)
```

```python
import functools

import jax
import jax.numpy as jnp
from jax import lax
from jax.experimental import pallas as pl
from jax.experimental.pallas import tpu as pltpu
from jax.sharding import PartitionSpec as P

HEAD_DIM = 128
SCALE = HEAD_DIM ** (-0.5)
LOG2E = 1.4426950408889634
HIDDEN_SCORE = -2e30
LOWEST = -1e30
CHUNK = 256
DOCS = 4
VMEM_BYTES = 48 * 1024 * 1024
bf16 = jnp.bfloat16
f32 = jnp.float32


def nt(a, b):
    return lax.dot_general(a, b, (((1,), (1,)), ((), ())), preferred_element_type=f32)


def nn(a, b):
    return lax.dot_general(a, b, (((1,), (0,)), ((), ())), preferred_element_type=f32)


def tn(a, b):
    return lax.dot_general(a, b, (((0,), (0,)), ((), ())), preferred_element_type=f32)


def sort_keys(order, kv, kvs, part):
    for b in range(kv.shape[0] // part):
        to = pl.multiple_of(order[b] * part, part)
        kvs[pl.ds(to, part), :] = kv[b * part : (b + 1) * part, :]


def stacked(qg, t, half, which):
    sources, _, width = qg.shape
    rows = slice((2 * which + t) * half, (2 * which + t + 1) * half)
    return jnp.concatenate(
        [qg[i, rows, n : n + HEAD_DIM] for i in range(sources) for n in range(0, width, HEAD_DIM)], axis=0
    )


def block_rows(outer, order, docs, t, part):
    half = docs.shape[1]
    block = order[2 * outer[0] + t]
    own = docs[pl.ds(block, 1), :]
    table = docs[...]
    first = jnp.zeros_like(own)
    for d in range(DOCS - 1):
        ones = (table == d).astype(jnp.int32)
        count = jnp.sum(jnp.sum(ones, axis=0, keepdims=True), axis=1, keepdims=True)
        first = first + jnp.where(own > d, count, 0)
    places = block * half + lax.broadcasted_iota(jnp.int32, (1, half), 1)
    low = (jnp.min(first) // half) * part // CHUNK
    high = (block * part + part - 1) // CHUNK + 1
    return places, first, low, high


def chunk_bias(inner, places, first, c, used, part, heads):
    half = places.shape[1]
    n = c * CHUNK + lax.broadcasted_iota(jnp.int32, (CHUNK, half), 0)
    keys = (n // part) * half + part * inner[0] + n % part
    seen = (keys <= jnp.where(used, places, -1)) & (keys >= first)
    bias = jnp.where(seen, 0.0, HIDDEN_SCORE)
    return jnp.concatenate([bias] * heads, axis=1)


def forward_kernel(part, inner, outer, order, docs, qg, kv, stats, low, kvs):
    sort_keys(order, kv, kvs, part)
    both = [block_rows(outer, order, docs, t, part) for t in range(2)]
    half = docs.shape[1]
    columns = stats.shape[-1] // 2
    heads = columns // half
    stats[...] = jnp.zeros_like(stats)
    rank, rows = low.shape
    total_low = qg[0, qg.shape[1] - rank :, :HEAD_DIM].astype(f32)
    for i in range(1, qg.shape[0]):
        total_low = total_low + qg[i, qg.shape[1] - rank :, :HEAD_DIM].astype(f32)
    low[...] = total_low[:, :rows]
    steps = jnp.maximum(both[0][3] - both[0][2], both[1][3] - both[1][2])

    def body(n, carried):
        out = []
        for t in range(2):
            places, first, low_chunk, high = both[t]
            peak, total, dot = carried[t]
            used = low_chunk + n < high
            c = jnp.minimum(low_chunk + n, high - 1)
            at = pl.multiple_of(c * CHUNK, CHUNK)
            k = kvs[pl.ds(at, CHUNK), :HEAD_DIM]
            v = kvs[pl.ds(at, CHUNK), HEAD_DIM:]
            bias = chunk_bias(inner, places, first, c, used, part, heads)
            s = nt(k, stacked(qg, t, half, 0)) * (SCALE * LOG2E) + bias
            dp = nt(v, stacked(qg, t, half, 1))
            new = jnp.maximum(peak, jnp.max(s, axis=0, keepdims=True))
            w = jnp.exp2(s - new)
            factor = jnp.exp2(peak - new)
            total = total * factor + jnp.sum(w, axis=0, keepdims=True)
            dot = dot * factor + jnp.sum(w * dp, axis=0, keepdims=True)
            out.append((new, total, dot))
        return tuple(out)

    zero = jnp.zeros((1, columns), f32)
    found = lax.fori_loop(0, steps, body, ((zero + LOWEST, zero, zero),) * 2)
    for t in range(2):
        for row, value in enumerate(found[t]):
            stats[row : row + 1, t * columns : (t + 1) * columns] = value


def row_terms(stats, t, columns):
    sources = stats.shape[0]
    span = slice(t * columns, (t + 1) * columns)
    peaks = [stats[i, 0:1, span] for i in range(sources)]
    peak = functools.reduce(jnp.maximum, peaks)
    factors = [jnp.exp2(p - peak) for p in peaks]
    total = sum(stats[i, 1:2, span] * factors[i] for i in range(sources))
    dot = sum(stats[i, 2:3, span] * factors[i] for i in range(sources))
    return peak + jnp.log2(total), dot / total


def key_kernel(part, inner, outer, order, docs, qg, kv, stats, dkv, kvs, acc):
    sort_keys(order, kv, kvs, part)
    both = [block_rows(outer, order, docs, t, part) for t in range(2)]
    half = docs.shape[1]
    columns = stats.shape[-1] // 2
    heads = columns // half
    acc[...] = jnp.zeros_like(acc)
    terms = [row_terms(stats, t, columns) for t in range(2)]
    steps = jnp.maximum(both[0][3] - both[0][2], both[1][3] - both[1][2])

    def body(n, carried):
        found = []
        for t in range(2):
            places, first, low_chunk, high = both[t]
            lse, delta = terms[t]
            used = low_chunk + n < high
            c = jnp.minimum(low_chunk + n, high - 1)
            at = pl.multiple_of(c * CHUNK, CHUNK)
            k = kvs[pl.ds(at, CHUNK), :HEAD_DIM]
            v = kvs[pl.ds(at, CHUNK), HEAD_DIM:]
            bias = chunk_bias(inner, places, first, c, used, part, heads)
            q = stacked(qg, t, half, 0)
            g = stacked(qg, t, half, 1)
            p = jnp.exp2(nt(k, q) * (SCALE * LOG2E) + bias - lse)
            ds = (p * (nt(v, g) - delta)).astype(bf16)
            found.append((at, nn(ds, q), nn(p.astype(bf16), g)))
        for at, dk, dv in found:
            acc[pl.ds(at, CHUNK), :HEAD_DIM] += dk
            acc[pl.ds(at, CHUNK), HEAD_DIM:] += dv
        return carried

    lax.fori_loop(0, steps, body, 0)
    for z in range(dkv.shape[0]):
        for t in range(2):
            at = pl.multiple_of(order[2 * z + t] * part, part)
            dkv[z, t * part : (t + 1) * part, :] = acc[pl.ds(at, part), :].astype(bf16)


def query_kernel(part, inner, outer, order, docs, qg, kv, stats, dq, kvs, dqt):
    sort_keys(order, kv, kvs, part)
    both = [block_rows(outer, order, docs, t, part) for t in range(2)]
    half = docs.shape[1]
    columns = stats.shape[-1] // 2
    heads = columns // half
    grp = heads // stats.shape[0]
    for t in range(2):
        places, first, low_chunk, high = both[t]
        lse, delta = row_terms(stats, t, columns)
        dqt[...] = jnp.zeros_like(dqt)

        def body(c, carried, t=t, places=places, first=first, lse=lse, delta=delta):
            at = pl.multiple_of(c * CHUNK, CHUNK)
            k = kvs[pl.ds(at, CHUNK), :HEAD_DIM]
            v = kvs[pl.ds(at, CHUNK), HEAD_DIM:]
            s = nt(k, stacked(qg, t, half, 0)) * (SCALE * LOG2E) + chunk_bias(inner, places, first, c, True, part, heads)
            dqt[...] += tn(k, (jnp.exp2(s - lse) * (nt(v, stacked(qg, t, half, 1)) - delta)).astype(bf16))
            return carried

        lax.fori_loop(low_chunk, high, body, 0)
        for h in range(heads):
            i, n = divmod(h, grp)
            dq[i, t * half : (t + 1) * half, n * HEAD_DIM : (n + 1) * HEAD_DIM] = (
                dqt[:, h * half : (h + 1) * half].T.astype(bf16)
            )


def input_kernel(
    part, inner, hidden_, at_, queries, grad_out, keys, values, qg, kv, hidden, at, low, wide, mixed, arrived
):
    sources, _, width = qg.shape
    tokens = queries.shape[0]
    half = tokens // 2
    pairs = [(queries, wide.at[:tokens, :]), (grad_out, wide.at[tokens:, :]), (hidden_, hidden), (at_, at)]
    for t in range(2):
        here = pl.multiple_of(t * half + inner[0] * part, part)
        to = slice(t * part, (t + 1) * part)
        pairs += [(keys.at[pl.ds(here, part), :], mixed.at[to, :HEAD_DIM])]
        pairs += [(values.at[pl.ds(here, part), :], mixed.at[to, HEAD_DIM:])]
    copies = [pltpu.make_async_copy(source, target, arrived.at[n]) for n, (source, target) in enumerate(pairs)]
    for copy in copies:
        copy.start()
    pairs = [(wide, qg.at[i, : 2 * tokens, :]) for i in range(sources)] + [(mixed, kv)]
    last = [
        pltpu.make_async_copy(source, target, arrived.at[len(copies) + n]) for n, (source, target) in enumerate(pairs)
    ]
    for copy in copies[:2]:
        copy.wait()
    for copy in last[:-1]:
        copy.start()
    for copy in copies[4:]:
        copy.wait()
    last[-1].start()
    for copy in copies[2:4]:
        copy.wait()
    whole = nt(at[...], hidden[...])
    empty = jnp.zeros((whole.shape[0], width - 2 * part), f32)
    for i in range(sources):
        mine = [whole[:, t * half + i * part : t * half + (i + 1) * part] for t in range(2)]
        low[i] = jnp.concatenate(mine + [empty], axis=1).astype(bf16)
    for i in range(sources):
        copy = pltpu.make_async_copy(low.at[i], qg.at[i, 2 * tokens :, :], arrived.at[len(copies) + len(pairs) + i])
        copy.start()
        last.append(copy)
    for copy in last:
        copy.wait()


def home_kernel(parts, ab, low, dkv, payload):
    total = parts[0].astype(f32)
    for o in range(1, parts.shape[0]):
        total = total + parts[o].astype(f32)
    dk = (total[:, :HEAD_DIM] * SCALE).astype(bf16)
    dkv[:, :HEAD_DIM] = dk
    dkv[:, HEAD_DIM:] = total[:, HEAD_DIM:].astype(bf16)
    back = nt(ab[...], dk)
    rank, rows = back.shape
    whole = jnp.concatenate([back, low[...]], axis=1).astype(bf16)
    for o in range(payload.shape[0]):
        payload[o] = whole


def adapter_kernel(inner_size, parts, dkv, hidden, payload):
    heads = parts.shape[0] // inner_size
    rows = hidden.shape[0] // inner_size
    piece = rows // 2
    half = hidden.shape[0] // 2
    ga = None
    gb = None
    for i in range(inner_size):
        both = parts[i].astype(f32)
        for h in range(1, heads):
            both = both + parts[h * inner_size + i].astype(f32)
        both = both.astype(bf16)
        here, there = i * piece, half + i * piece
        mine = jnp.concatenate([hidden[here : here + piece, :], hidden[there : there + piece, :]], axis=0)
        term = nn(both[:, :rows], mine)
        ga = term if ga is None else ga + term
        term = nn(both[:, rows:], dkv[i * rows : (i + 1) * rows, :HEAD_DIM])
        gb = term if gb is None else gb + term
    whole = jnp.concatenate([ga, gb], axis=1).astype(bf16)
    for o in range(payload.shape[0]):
        payload[o] = whole


def final_kernel(parts, ga, gb):
    total = parts[0].astype(f32)
    for o in range(1, parts.shape[0]):
        total = total + parts[o].astype(f32)
    width = ga.shape[1]
    ga[...] = total[:, :width]
    gb[...] = total[:, width:]


def call(kernel, out_shape, specs, scratch=(), cost=None, vmem=VMEM_BYTES, outs=None):
    spaces = {"s": pltpu.SMEM, "v": pltpu.VMEM, "h": pltpu.HBM}
    single = not isinstance(out_shape, tuple)
    return pl.pallas_call(
        kernel,
        out_shape=out_shape,
        in_specs=[pl.BlockSpec(memory_space=spaces[s]) for s in specs],
        out_specs=pl.BlockSpec(memory_space=pltpu.VMEM)
        if single
        else tuple(pl.BlockSpec(memory_space=spaces[o]) for o in outs or "v" * len(out_shape)),
        scratch_shapes=list(scratch),
        compiler_params=pltpu.CompilerParams(vmem_limit_bytes=vmem),
        cost_estimate=cost,
    )


def on_device(queries, keys, values, grad_out, hidden_in, adapter_a, adapter_b, block_order, doc_ids):
    sd = jax.ShapeDtypeStruct
    n_outer, n_inner, n_head = lax.axis_size("outer"), lax.axis_size("inner"), lax.axis_size("head")
    outer, inner = lax.axis_index("outer"), lax.axis_index("inner")
    tokens = queries.shape[0]
    half = tokens // 2
    part = half // n_inner
    rows = 2 * part
    heads = n_inner * queries.shape[1] // HEAD_DIM
    columns = heads * half
    total_rows = n_outer * rows
    rank = adapter_b.shape[0]

    width = hidden_in.shape[1]
    docs = doc_ids.reshape(-1, half)
    ids = (inner.astype(jnp.int32)[None], outer.astype(jnp.int32)[None], block_order)
    qg, kv = call(
        functools.partial(input_kernel, part),
        (
            sd((n_inner, 2 * tokens + rank, queries.shape[1]), bf16),
            sd((rows, 2 * HEAD_DIM), bf16),
        ),
        "shhhhhh",
        [
            pltpu.VMEM(hidden_in.shape, bf16),
            pltpu.VMEM((rank, width), bf16),
            pltpu.VMEM((n_inner, rank, queries.shape[1]), bf16),
            pltpu.VMEM((2 * tokens, queries.shape[1]), bf16),
            pltpu.VMEM((rows, 2 * HEAD_DIM), bf16),
            pltpu.SemaphoreType.DMA((9 + 2 * n_inner,)),
        ],
        vmem=None,
        outs="hh",
    )(ids[0], hidden_in, adapter_a.T, queries, grad_out, keys, values)
    qg = lax.all_to_all(qg, "inner", 0, 0, tiled=True)
    kv = lax.all_gather(kv, "outer", axis=0, tiled=True)

    staged = [
        pltpu.VMEM((total_rows, 2 * HEAD_DIM), bf16),
    ]
    pair = 2 * columns * total_rows * HEAD_DIM
    stats, low = call(
        functools.partial(forward_kernel, part),
        (sd((4, 2 * columns), f32), sd((rank, rows), f32)),
        "sssvvv",
        staged,
        pl.CostEstimate(flops=2 * pair, bytes_accessed=2 << 20, transcendentals=columns * total_rows),
    )(*ids, docs, qg, kv)
    stats = lax.all_gather(stats, "inner", axis=0, tiled=False)
    dkv = call(
        functools.partial(key_kernel, part),
        sd((n_outer, rows, 2 * HEAD_DIM), bf16),
        "sssvvvv",
        staged + [pltpu.VMEM((total_rows, 2 * HEAD_DIM), f32)],
        pl.CostEstimate(flops=4 * pair, bytes_accessed=3 << 20, transcendentals=columns * total_rows),
    )(*ids, docs, qg, kv, stats)
    dkv, stats = lax.optimization_barrier((dkv, stats))
    dq = call(
        functools.partial(query_kernel, part),
        sd((n_inner, tokens, queries.shape[1]), bf16),
        "sssvvvv",
        staged + [pltpu.VMEM((HEAD_DIM, columns), f32)],
        pl.CostEstimate(flops=3 * pair, bytes_accessed=3 << 20, transcendentals=columns * total_rows),
    )(*ids, docs, qg, kv, stats)

    home = lax.all_to_all(dkv, "outer", 0, 0, tiled=True)
    own = lax.dynamic_index_in_dim(dq, inner, 0, keepdims=False).astype(f32)
    for d in range(1, n_inner):
        sent = lax.dynamic_index_in_dim(dq, inner ^ d, 0, keepdims=False)
        own = own + lax.ppermute(sent, "inner", [(i, i ^ d) for i in range(n_inner)]).astype(f32)
    grad_query = (own * SCALE).astype(bf16)

    home, grad_query = lax.optimization_barrier((home, grad_query))
    dkv, payload = call(
        home_kernel,
        (sd((rows, 2 * HEAD_DIM), bf16), sd((n_head * n_inner, rank, 2 * rows), bf16)),
        "vvv",
    )(home, adapter_b, low)
    payload = lax.all_to_all(payload, ("head", "inner"), 0, 0, tiled=True)
    dkv = lax.all_gather(dkv, "inner", axis=0, tiled=True)
    payload = call(
        functools.partial(adapter_kernel, n_inner), sd((n_outer, rank, width + HEAD_DIM), bf16), "vvv"
    )(payload, dkv, hidden_in)
    payload = lax.all_to_all(payload, "outer", 0, 0, tiled=True)

    dkv = dkv.reshape(n_inner, 2, part, 2 * HEAD_DIM).transpose(1, 0, 2, 3).reshape(tokens, 2 * HEAD_DIM)
    grad_key, grad_value = dkv[:, :HEAD_DIM], dkv[:, HEAD_DIM:]
    payload, grad_query, grad_key, grad_value = lax.optimization_barrier(
        (payload, grad_query, grad_key, grad_value)
    )
    grad_a, grad_b = call(final_kernel, (sd((rank, width), f32), sd((rank, HEAD_DIM), f32)), "v")(payload)
    return grad_query, grad_key, grad_value, grad_a.T, grad_b


def solution(mesh):
    in_specs = (
        P("outer", ("head", "inner")),
        P("outer", "head"),
        P("outer", "head"),
        P("outer", ("head", "inner")),
        P("outer", ("head", "inner")),
        P(("head", "inner"), None),
        P(None, "head"),
        P(),
        P(),
    )
    out_specs = (
        P("outer", ("head", "inner")),
        P("outer", "head"),
        P("outer", "head"),
        P(("head", "inner"), None),
        P(None, "head"),
    )
    return jax.shard_map(on_device, mesh=mesh, in_specs=in_specs, out_specs=out_specs, check_vma=False)
```
